32 devices in a mesh: tile: 8 (over z, core), depth: 4 (over y, x).
Axes of the slice: x: 2, y: 2, z: 4, core: 2. Of those that a mesh axis runs over, the one named last changes fastest.
Arguments:
- velocity: float32 [3, 32, 64, 128], P(None, 'tile', 'depth'), may hold values from -6 to 6
- stress: float32 [6, 32, 64, 128], P(None, 'tile', 'depth'), may hold values from -6 to 6
- memory: float32 [18, 32, 64, 128], P(None, 'tile', 'depth'), may hold values from -3 to 3
- buoyancy: float32 [32, 64, 128], P('tile', 'depth'), may hold values from 0.5 to 1.5
- lame: float32 [2, 32, 64, 128], P(None, 'tile', 'depth'), may hold values from 0.5 to 1.5
- qinv: float32 [2, 32, 64, 128], P(None, 'tile', 'depth'), may hold values from 0.05 to 0.5
- relax: float32 [3], replicated, may hold values from 0.1 to 0.9
- fwd_strain: bfloat16 [4, 6, 32, 64, 128], P(None, None, 'tile', 'depth'), may hold values from -6 to 6
- residual: float32 [32, 3, 1024], P(None, None, 'tile'), may hold values from -6 to 6
- station_owner: int32 [1024, 1], P('tile'), may hold values from 0 to 7; in each aligned block of 128 rows (0 to 127, 128 to 255, ...) at most 64 rows name the same one
- station_cell: int32 [1024], P('tile'), may hold values from 0 to 511
- time_index: int32 [4], replicated, may hold values from 0 to 31
Outputs:
- velocity_out: float32 [3, 32, 64, 128], P(None, 'tile', 'depth')
- stress_out: float32 [6, 32, 64, 128], P(None, 'tile', 'depth')
- memory_out: float32 [18, 32, 64, 128], P(None, 'tile', 'depth')
- kernel_q: float32 [32, 64, 128], P('tile', 'depth')
The draws below stay inside these ranges and needn't reach their ends.
Inputs may be any that keep to these rules, and one draw needn't show every extreme that they name: `station_owner`: in each aligned block of 128 stations (the stations of one tile index) no tile is named by more than 64 stations, a bound that some block reaches; every tile is named by some station.
All inputs are finite; a program needn't handle non-finite values.
Results may differ from the reference program's by a relative error of at most 0.0004.
Values sent between devices are 32-bit elements; how exact they have to be, the bound alone decides.
A program may use at most 64 MiB of HBM per device.

```python
import math
import jax
import jax.numpy as jnp
import numpy as np
from jax import lax

CX = 4
NY = 128
STA_DEV = 128
SAMPLES = 32
STEPS = 4
MECH = 3
NX = 32
NZ = 64
STATIONS = 1024
CAP = 64
N_TILE = 8


def touch_ends(values, own_key, low, top_value):
    shape = values.shape
    index_at = [jax.random.randint(jax.random.fold_in(own_key, axis), (), 0, shape[axis]) for axis in range(len(shape))]
    values = values.at[tuple(index_at)].set(low)
    longest = shape.index(max(shape))
    index_at[longest] = (index_at[longest] + 1) % shape[longest]
    return values.at[tuple(index_at)].set(top_value)


def shard_levels(own_key, shape, shards, least, largest):
    level, own = 1.0, jax.random.fold_in(own_key, 6)
    for dim, shards_of in shards:
        steps = jnp.exp(jax.random.uniform(jax.random.fold_in(own, dim), (shards_of,), jnp.float32, least / len(shards), largest / len(shards)))
        level = level * jnp.repeat(steps, shape[dim] // shards_of).reshape([-1 if axis == dim else 1 for axis in range(len(shape))])
    return level


def shared_out(stream_key, own, number, rows, number_of, top, most, lean):
    order = jax.random.permutation(stream_key, number_of)
    packed, common = portions_of(number_of, rows * top, most, lean, True), portions_of(number_of, rows * top, most, lean, False)
    places = jnp.arange(number_of)

    def named(tallies, offset_by):
        used = int((tallies > 0).sum())
        fixed = max(1, used // 4)
        shifted = fixed + (places - fixed + offset_by * (used - fixed)) % max(1, number_of - fixed)
        return jnp.zeros((number_of,), jnp.int32).at[order[jnp.where(places < fixed, places, shifted)]].set(jnp.asarray(tallies, jnp.int32))

    tallies = jnp.where(number % 4 == 0, named(packed, number // 4), named(common, number - number // 4 - 1))
    mixed = jax.random.permutation(jax.random.fold_in(own, 3), number_of)
    giver, sink = mixed[0:number_of // 2 * 2:2], mixed[1:number_of // 2 * 2:2]
    margin = jnp.minimum(tallies[giver] - 1, most - tallies[sink]) // 2
    margin = jnp.where((giver == order[0]) | (sink == order[0]) | (tallies[sink] == 0), 0, jnp.maximum(margin, 0))
    shifted = jax.random.randint(jax.random.fold_in(own, 4), (number_of // 2,), 0, 1 << 20) % (margin + 1)
    tallies = tallies.at[giver].add(-shifted).at[sink].add(shifted)
    members = jnp.searchsorted(jnp.cumsum(tallies), jnp.arange(rows * top), side="right").astype(jnp.int32)
    grid = members.reshape(top, rows).T
    grid = grid[jax.random.permutation(jax.random.fold_in(own, 1), rows)]
    offset_by = jax.random.randint(jax.random.fold_in(own, 2), (rows, 1), 0, top)
    return jnp.take_along_axis(grid, (jnp.arange(top)[None, :] + offset_by) % top, axis=1)


def portions_of(number_of, total, limit, lean, full):
    portions = [(1 << 20) // math.isqrt(grade ** lean) + 1 for grade in range(1, number_of + 1)]
    largest = limit if full else min(limit, max(-(-total // number_of), total * portions[0] // sum(portions)))
    least = 1 if total - largest >= number_of - 1 else 0
    counts, spare = [largest] + [least] * (number_of - 1), total - largest - least * (number_of - 1)
    while spare > 0:
        movable = [i for i in range(1, number_of) if counts[i] < largest] or [i for i in range(1, number_of) if counts[i] < limit]
        pool, budget = sum([portions[i] for i in movable]), spare
        for i in movable:
            more = min(limit - counts[i], max(1, budget * portions[i] // pool), spare)
            counts[i] = counts[i] + more
            spare = spare - more
    return np.array(counts)


def gaussian(own_key, extent, scale, reach, shards=(), kind=jnp.bfloat16):
    values = jax.random.normal(own_key, extent, jnp.float32) * scale
    if len(shards) > 0:
        values = shard_levels(own_key, extent, shards, -0.22, 0.18) * values
    return jnp.clip(values, min=-reach, max=reach).astype(kind)


def setup_inputs(seed: int = 0) -> dict:
    streams_of = jax.random.split(jax.random.key(seed), 13)
    velocity = gaussian(streams_of[0], (3, NX, NZ, NY), 1.0, 6.0, ((1, 8), (2, 4)), jnp.float32)
    stress = gaussian(streams_of[1], (6, NX, NZ, NY), 1.0, 6.0, ((1, 8), (2, 4)), jnp.float32)
    memory = gaussian(streams_of[2], (6 * MECH, NX, NZ, NY), 0.5, 3.0, ((1, 8), (2, 4)), jnp.float32)
    buoyancy = jnp.clip(0.5 + 1.0 * jax.random.uniform(streams_of[3], (NX, NZ, NY), jnp.float32) ** shard_levels(streams_of[3], (NX, NZ, NY), ((0, 8), (1, 4)), -0.2, 0.2), 0.5, 1.5)
    lame = jnp.clip(0.5 + 1.0 * jax.random.uniform(streams_of[4], (2, NX, NZ, NY), jnp.float32) ** shard_levels(streams_of[4], (2, NX, NZ, NY), ((1, 8), (2, 4)), -0.2, 0.2), 0.5, 1.5)
    qinv = jnp.clip(jnp.exp(math.log(0.5) - 2.3025851 * jax.random.uniform(streams_of[5], (2, NX, NZ, NY), jnp.float32) ** shard_levels(streams_of[5], (2, NX, NZ, NY), ((1, 8), (2, 4)), -0.2, 0.2)), 0.05, 0.5)
    relax = jnp.clip(jax.random.uniform(streams_of[6], (MECH,), jnp.float32, 0.1, 0.9), 0.1, 0.9)
    fwd_strain = gaussian(streams_of[7], (STEPS, 6, NX, NZ, NY), 1.0, 6.0, ((2, 8), (3, 4)))
    residual = gaussian(streams_of[8], (SAMPLES, 3, STATIONS), 1.0, 6.0, ((2, 8),), jnp.float32)
    station_owner_keys = jax.random.split(jax.random.fold_in(streams_of[9], 1), STATIONS // STA_DEV)
    station_owner_turns = jax.random.permutation(jax.random.fold_in(streams_of[9], 3), STATIONS // STA_DEV)
    station_owner = jax.vmap(lambda own, number: shared_out(jax.random.fold_in(streams_of[9], 2), own, number, STA_DEV, N_TILE, 1, CAP, 2))(station_owner_keys, station_owner_turns).reshape((STATIONS, 1))
    station_cell = touch_ends(jax.random.randint(streams_of[10], (STATIONS,), 0, CX * NY), jax.random.fold_in(streams_of[10], 1), 0, (CX * NY) - 1).astype(jnp.int32)
    time_index = touch_ends(jax.random.randint(streams_of[11], (STEPS,), 0, SAMPLES), jax.random.fold_in(streams_of[11], 1), 0, SAMPLES - 1).astype(jnp.int32)
    return dict(velocity=velocity, stress=stress, memory=memory, buoyancy=buoyancy, lame=lame, qinv=qinv, relax=relax, fwd_strain=fwd_strain, residual=residual, station_owner=station_owner, station_cell=station_cell, time_index=time_index)


courant = 0.2
mech_weights = (2.0, 3.0, 4.0)


def differ(field, axis):
    widths = [(0, 0)] * field.ndim
    widths[axis] = (1, 1)
    padded = jnp.pad(field, widths)
    count = field.shape[axis]
    return 0.5 * (lax.slice_in_dim(padded, 2, count + 2, axis=axis) - lax.slice_in_dim(padded, 0, count, axis=axis))


def reference(velocity, stress, memory, buoyancy, lame, qinv, relax, fwd_strain, residual, station_owner, station_cell, time_index):
    lam = lame[0]
    shear = lame[1]
    kappa = lam + (2.0 / 3.0) * shear
    diagonal = jnp.array([1.0, 1.0, 1.0, 0.0, 0.0, 0.0], dtype=velocity.dtype).reshape(6, 1, 1, 1)
    weights = jnp.array(mech_weights, dtype=velocity.dtype)
    flat = (station_owner[:, 0] * (CX * NY) + station_cell).astype(jnp.int32)
    kernel = jnp.zeros(buoyancy.shape, velocity.dtype)
    for step in range(STEPS):
        rows = jnp.take(residual, time_index[step], axis=0)
        inject = jnp.zeros((3, NX * NY), velocity.dtype).at[:, flat].add(rows).reshape(3, NX, NY)
        velocity = velocity.at[:, :, 0, :].add(buoyancy[None, :, 0, :] * inject)
        sx = differ(stress, 1)
        sz = differ(stress, 2)
        sy = differ(stress, 3)
        diverge = jnp.stack([sx[0] + sy[3] + sz[4], sx[3] + sy[1] + sz[5], sx[4] + sy[5] + sz[2]])
        velocity = velocity + courant * buoyancy[None] * diverge
        gx = differ(velocity, 1)
        gz = differ(velocity, 2)
        gy = differ(velocity, 3)
        strain = jnp.stack([gx[0], gy[1], gz[2], 0.5 * (gy[0] + gx[1]), 0.5 * (gz[0] + gx[2]), 0.5 * (gz[1] + gy[2])])
        theta = strain[0] + strain[1] + strain[2]
        deviator = strain - diagonal * (theta / 3.0)[None]
        force = 2.0 * shear[None] * qinv[0][None] * deviator + diagonal * (kappa * qinv[1] * theta)[None]
        mems = memory.reshape(MECH, 6, NX, NZ, NY)
        keep = (1.0 - relax).reshape(MECH, 1, 1, 1, 1)
        push = (relax * weights).reshape(MECH, 1, 1, 1, 1)
        mems = keep * mems - push * force[None]
        stress = stress + courant * (diagonal * (lam * theta)[None] + 2.0 * shear[None] * strain + jnp.sum(mems, axis=0))
        kernel = kernel + courant * jnp.sum(mems * fwd_strain[step].astype(velocity.dtype)[None], axis=(0, 1))
        memory = mems.reshape(MECH * 6, NX, NZ, NY)
    return velocity, stress, memory, kernel
```

```python
import functools

import jax
import jax.numpy as jnp
from jax import lax
from jax.experimental import pallas as pl
from jax.experimental.pallas import tpu as pltpu
from jax.sharding import PartitionSpec as P

courant = 0.2
mech_weights = (2.0, 3.0, 4.0)
MESH = pl.DeviceIdType.MESH

x_comps = (0, 3, 4)
z_comps = (4, 5, 2)
y_comps = (3, 1, 5)
corner_comps = (0, 3, 4, 5, 2)
step_of = (-1, 1)


def steps_kernel(
    n_tile,
    n_depth,
    relax,
    time_index,
    stress_in,
    velocity_in,
    buoyancy_in,
    owner_in,
    cell_in,
    residual_in,
    lame_in,
    qinv_in,
    memory_in,
    fwd_in,
    velocity_out,
    stress_out,
    memory_out,
    kernel_out,
    stress,
    velocity,
    buoyancy,
    owner,
    cell,
    residual,
    lame,
    qinv,
    memory,
    fwd,
    coef,
    force,
    kern,
    inject,
    gathered,
    xs,
    zs,
    cs,
    xr,
    zr,
    cr,
    in_sem,
    out_sem,
    gs_sem,
    gr_sem,
    xs_sem,
    xr_sem,
    zs_sem,
    zr_sem,
    cs_sem,
    cr_sem,
):
    steps = fwd.shape[0]
    mechs = memory.shape[0] // 6
    cx, cz, ny = velocity.shape[1:]
    listed = owner.shape[1]
    my_t = lax.axis_index("tile")
    my_d = lax.axis_index("depth")

    loads = []
    for number, (src, dst) in enumerate(
        (
            (stress_in, stress),
            (velocity_in, velocity),
            (buoyancy_in, buoyancy),
            (owner_in, owner),
            (cell_in, cell),
            (residual_in, residual),
            (lame_in, lame),
            (qinv_in, qinv),
            (memory_in, memory),
            (fwd_in, fwd),
        )
    ):
        copy = pltpu.make_async_copy(src, dst, in_sem.at[number])
        copy.start()
        loads.append(copy)

    has_t = (my_t > 0, my_t < n_tile - 1)
    has_d = (my_d > 0, my_d < n_depth - 1)
    top = my_d == 0

    barrier = pltpu.get_barrier_semaphore()

    def greet(device, amount=1):
        pl.semaphore_signal(barrier, inc=amount, device_id=device, device_id_type=MESH)

    meets = []
    for other in range(2):
        meets.append((has_d[other], my_t, my_d + step_of[other]))
        for side in range(2):
            meets.append(
                (
                    jnp.logical_and(has_t[side], has_d[other]),
                    my_t + step_of[side],
                    my_d + step_of[other],
                )
            )
    for side in range(2):
        meets.append(
            (jnp.logical_and(has_t[side], jnp.logical_not(top)), my_t + step_of[side], my_d)
        )
    for here, to_t, to_d in meets:
        pl.when(here)(lambda: greet((to_t, to_d)))

    @pl.when(top)
    def _():
        for hop in range(1, n_tile):
            greet((lax.rem(my_t + hop, n_tile), my_d))

    for side in range(2):

        @pl.when(jnp.logical_not(has_t[side]))
        def _():
            xr[:, side] = jnp.zeros((steps, 7, cz, ny), jnp.float32)

        @pl.when(jnp.logical_not(has_d[side]))
        def _():
            zr[:, side] = jnp.zeros((steps, 7, cx, 1, ny), jnp.float32)

        for other in range(2):

            @pl.when(jnp.logical_not(jnp.logical_and(has_t[side], has_d[other])))
            def _():
                cr[:, side, other] = jnp.zeros((steps, 5, 1, ny), jnp.float32)

    def gather_copy(hop):
        return pltpu.make_async_remote_copy(
            src_ref=gathered.at[0],
            dst_ref=gathered.at[hop],
            send_sem=gs_sem.at[hop],
            recv_sem=gr_sem.at[hop],
            device_id=(lax.rem(my_t + hop, n_tile), my_d),
            device_id_type=MESH,
        )

    def x_copy(step, side):
        comps = 7 if step == 0 else 6
        return pltpu.make_async_remote_copy(
            src_ref=xs.at[step, side, pl.ds(0, comps)],
            dst_ref=xr.at[step, 1 - side, pl.ds(0, comps)],
            send_sem=xs_sem.at[step, side],
            recv_sem=xr_sem.at[step, 1 - side],
            device_id=(my_t + step_of[side], my_d),
            device_id_type=MESH,
        )

    def z_copy(step, side):
        comps = 7 if step == 0 else 6
        return pltpu.make_async_remote_copy(
            src_ref=zs.at[step, side, pl.ds(0, comps)],
            dst_ref=zr.at[step, 1 - side, pl.ds(0, comps)],
            send_sem=zs_sem.at[step, side],
            recv_sem=zr_sem.at[step, 1 - side],
            device_id=(my_t, my_d + step_of[side]),
            device_id_type=MESH,
        )

    def corner_copy(step, side, other):
        return pltpu.make_async_remote_copy(
            src_ref=cs.at[step, side, other],
            dst_ref=cr.at[step, 1 - side, 1 - other],
            send_sem=cs_sem.at[step, side, other],
            recv_sem=cr_sem.at[step, 1 - side, 1 - other],
            device_id=(my_t + step_of[side], my_d + step_of[other]),
            device_id_type=MESH,
        )

    shape = (cx, cz, ny)
    at_z = lax.broadcasted_iota(jnp.int32, shape, 1)
    at_y = lax.broadcasted_iota(jnp.int32, shape, 2)
    z_first, z_last = at_z == 0, at_z == cz - 1
    y_first, y_last = at_y == 0, at_y == ny - 1
    ends_x = (0, cx - 1)
    ends_z = (0, cz - 1)

    def diff_y(field):
        after = jnp.where(y_last, 0.0, pltpu.roll(field, ny - 1, 2))
        before = jnp.where(y_first, 0.0, pltpu.roll(field, 1, 2))
        return after - before

    def diff_z(field, low, high):
        after = jnp.where(z_last, high, pltpu.roll(field, cz - 1, 1))
        before = jnp.where(z_first, low, pltpu.roll(field, 1, 1))
        return after - before

    def diff_x(field, low, high):
        return jnp.concatenate([field[1:], high], axis=0) - jnp.concatenate(
            [low, field[:-1]], axis=0
        )

    def send_corners(step):
        for side in range(2):
            for other in range(2):

                @pl.when(jnp.logical_and(has_t[side], has_d[other]))
                def _():
                    for slot, comp in enumerate(corner_comps):
                        cs[step, side, other, slot] = stress[
                            comp, ends_x[side], pl.ds(ends_z[other], 1), :
                        ]
                    corner_copy(step, side, other).start()

    def send_sides(step):
        scale = (0.5 * courant) * buoyancy[...]
        none_x = jnp.zeros((1, cz, ny), jnp.float32)
        for comp in range(3):
            sx = stress[x_comps[comp]]
            sz = stress[z_comps[comp]]
            change = (
                diff_x(sx, none_x, none_x)
                + diff_y(stress[y_comps[comp]])
                + diff_z(sz, 0.0, 0.0)
            )
            part = velocity[comp] + scale * change
            velocity[comp] = part
            for side in range(2):
                xs[step, side, comp] = part[ends_x[side]]
                xs[step, side, 3 + comp] = sx[ends_x[side]]
                end = ends_z[side]
                zs[step, side, comp] = part[:, end : end + 1, :]
                zs[step, side, 3 + comp] = sz[:, end : end + 1, :]
        if step == 0:
            for side in range(2):
                xs[step, side, 6] = scale[ends_x[side]]
                end = ends_z[side]
                zs[step, side, 6] = scale[:, end : end + 1, :]
        for side in range(2):
            pl.when(has_d[side])(lambda: z_copy(step, side).start())
            pl.when(has_t[side])(lambda: x_copy(step, side).start())

    def wait_halo(step):
        for side in range(2):
            pl.when(has_d[side])(lambda: z_copy(step, 1 - side).wait_recv())
            pl.when(has_t[side])(lambda: x_copy(step, 1 - side).wait_recv())
            for other in range(2):
                pl.when(jnp.logical_and(has_t[side], has_d[other]))(
                    lambda: corner_copy(step, 1 - side, 1 - other).wait_recv()
                )

    def wait_sent(step):
        for side in range(2):
            pl.when(has_d[side])(lambda: z_copy(step, side).wait_send())
            pl.when(has_t[side])(lambda: x_copy(step, side).wait_send())
            for other in range(2):
                pl.when(jnp.logical_and(has_t[side], has_d[other]))(
                    lambda: corner_copy(step, side, other).wait_send()
                )

    keeps = [1.0 - relax[mech] for mech in range(mechs)]
    pushes = [relax[mech] * mech_weights[mech] for mech in range(mechs)]
    push_all = pushes[0]
    for push in pushes[1:]:
        push_all = push_all + push

    peers = jnp.where(top, n_tile - 1, 0)
    for here, _, _ in meets:
        peers = peers + jnp.where(here, 1, 0)
    pl.semaphore_wait(barrier, peers)

    for number in (3, 4, 5):
        loads[number].wait()

    @pl.when(top)
    def _():
        gathered[0, 8:16] = jnp.zeros((8, listed), jnp.float32)
        for step in range(steps):
            gathered[0, 3 * step : 3 * step + 3] = residual[time_index[step]]
        gathered[0, 3 * steps : 3 * steps + 1] = (owner[...] * (cx * ny) + cell[...]).astype(
            jnp.float32
        )
        for hop in range(1, n_tile):
            gather_copy(hop).start()

    loads[0].wait()
    send_corners(0)
    loads[1].wait()
    loads[2].wait()
    send_sides(0)

    loads[6].wait()
    loads[7].wait()
    lam, shear = lame[0], lame[1]
    twist = 2.0 * shear
    shape_part = twist * qinv[0]
    bulk_part = (lam + (2.0 / 3.0) * shear) * qinv[1] - shape_part * (1.0 / 3.0)
    coef[0] = shape_part
    coef[1] = bulk_part
    kern[...] = jnp.zeros(shape, jnp.float32)

    @pl.when(top)
    def _():
        for hop in range(1, n_tile):
            gather_copy(hop).wait_recv()
        rows = jnp.concatenate([gathered[hop] for hop in range(n_tile)], axis=1)
        target = rows[3 * steps : 3 * steps + 1].astype(jnp.int32)
        total = n_tile * listed
        at_cell = lax.broadcasted_iota(jnp.int32, (ny, total), 0)
        hot = jnp.where(at_cell == lax.rem(target, ny), 1.0, 0.0).astype(jnp.bfloat16)
        local = target - (my_t * cx - 1) * ny
        high = rows.astype(jnp.bfloat16).astype(jnp.float32)
        rest = rows - high
        middle = rest.astype(jnp.bfloat16).astype(jnp.float32)
        low = rest - middle
        sides = []
        for part in (high, middle, low):
            for layer in range(cx + 2):
                inside = jnp.logical_and(local >= layer * ny, local < (layer + 1) * ny)
                sides.append(jnp.where(inside, part, 0.0).astype(jnp.bfloat16))
        found = lax.dot_general(
            jnp.concatenate(sides, axis=0),
            hot,
            (((1,), (1,)), ((), ())),
            preferred_element_type=jnp.float32,
        )
        third = (cx + 2) * 16
        found = found[:third] + found[third : 2 * third] + found[2 * third :]
        for layer in range(cx + 2):
            inject[layer] = found[16 * layer : 16 * layer + 16]

    @pl.when(jnp.logical_not(top))
    def _():
        inject[...] = jnp.zeros((cx + 2, 16, ny), jnp.float32)

    loads[8].wait()
    loads[9].wait()

    stores = []

    def store(src, dst):
        copy = pltpu.make_async_copy(src, dst, out_sem.at[len(stores)])
        copy.start()
        stores.append(copy)

    edge = lax.broadcasted_iota(jnp.int32, (1, cz, ny), 1)
    edge_ends = (edge == 0, edge == cz - 1)
    for step in range(steps):
        last = step == steps - 1
        base = []
        for comp in range(6):
            total = keeps[0] * memory[comp]
            for mech in range(1, mechs):
                total = total + keeps[mech] * memory[6 * mech + comp]
            base.append(total)
        for comp in range(6):
            force[comp] = base[comp]

        wait_halo(step)

        scale = (0.5 * courant) * buoyancy[...]
        x_scale = [xr[0, side, 6] for side in range(2)]
        z_scale = [zr[0, side, 6] for side in range(2)]
        grads_x, grads_y, grads_z = [], [], []
        for comp in range(3):
            own = velocity[comp]
            row = 3 * step + comp
            signs = (-1.0, 1.0)
            around_x, around_z = [], []
            extra = []
            for side in range(2):
                sx_end = stress[x_comps[comp], ends_x[side]]
                halo = xr[step, side, comp] - signs[side] * x_scale[side] * sx_end
                fix = jnp.zeros((cz, ny), jnp.float32)
                for other in range(2):
                    at_corner = cr[step, side, other, corner_comps.index(z_comps[comp])]
                    fix = fix + jnp.where(edge_ends[other][0], signs[other] * at_corner, 0.0)
                push_in = inject[(0, cx + 1)[side], row : row + 1, :] * (2.0 / courant)
                fix = fix + jnp.where(edge_ends[0][0], push_in, 0.0)
                around_x.append((halo + x_scale[side] * fix)[None])
                extra.append((signs[side] * xr[step, side, 3 + comp])[None])

                sz_end = stress[z_comps[comp], :, pl.ds(ends_z[side], 1), :]
                corner_row = corner_comps.index(x_comps[comp])
                at_low = cr[step, 0, side, corner_row][None]
                at_high = cr[step, 1, side, corner_row][None]
                middle = jnp.zeros((cx - 2, 1, ny), jnp.float32)
                if cx > 1:
                    fix = jnp.concatenate([-at_low, middle, at_high], axis=0)
                else:
                    fix = at_high - at_low
                around_z.append(
                    zr[step, side, comp] + z_scale[side] * (fix - signs[side] * sz_end)
                )
            if cx > 1:
                change = jnp.concatenate(
                    [extra[0], jnp.zeros((cx - 2, cz, ny), jnp.float32), extra[1]], axis=0
                )
            else:
                change = extra[0] + extra[1]
            push_in = inject[1 : cx + 1, row : row + 1, :] * (2.0 / courant)
            change = change + jnp.where(z_first, push_in - zr[step, 0, 3 + comp], 0.0)
            change = change + jnp.where(z_last, zr[step, 1, 3 + comp], 0.0)
            own = own + scale * change
            velocity[comp] = own
            grads_x.append(diff_x(own, around_x[0], around_x[1]))
            grads_y.append(diff_y(own))
            grads_z.append(diff_z(own, around_z[0], around_z[1]))
        if last:
            store(velocity, velocity_out)
        strain = [
            0.5 * grads_x[0],
            0.5 * grads_y[1],
            0.5 * grads_z[2],
            0.25 * (grads_y[0] + grads_x[1]),
            0.25 * (grads_z[0] + grads_x[2]),
            0.25 * (grads_z[1] + grads_y[2]),
        ]
        theta = strain[0] + strain[1] + strain[2]
        bulk = coef[1] * theta
        pressure = lame[0] * theta
        weighted = kern[...]
        for comp in range(6):
            push = coef[0] * strain[comp]
            grow = 2.0 * lame[1] * strain[comp]
            if comp < 3:
                push = push + bulk
                grow = grow + pressure
            total = force[comp] - push_all * push
            force[comp] = push
            stress[comp] = stress[comp] + courant * (grow + total)
            weighted = weighted + total * fwd[step, comp].astype(jnp.float32)
        if last:
            store(stress, stress_out)
            kern[...] = courant * weighted
            store(kern, kernel_out)
        else:
            kern[...] = weighted
            send_corners(step + 1)
            send_sides(step + 1)
        for mech in range(mechs):
            for comp in range(6):
                index = 6 * mech + comp
                memory[index] = keeps[mech] * memory[index] - pushes[mech] * force[comp]
            if last:
                rows = pl.ds(6 * mech, 6)
                store(memory.at[rows], memory_out.at[rows])

    for step in range(steps):
        wait_sent(step)

    @pl.when(top)
    def _():
        for hop in range(1, n_tile):
            gather_copy(hop).wait_send()

    for copy in stores:
        copy.wait()


def per_device(
    n_tile,
    n_depth,
    velocity,
    stress,
    memory,
    buoyancy,
    lame,
    qinv,
    relax,
    fwd_strain,
    residual,
    station_owner,
    station_cell,
    time_index,
):
    steps = fwd_strain.shape[0]
    mechs = relax.shape[0]
    cx, cz, ny = buoyancy.shape
    listed = station_cell.shape[0]
    f32 = jnp.float32
    owner = station_owner.reshape(1, listed)
    cell = station_cell.reshape(1, listed)
    any_spec = pl.BlockSpec(memory_space=pl.ANY)
    smem_spec = pl.BlockSpec(memory_space=pltpu.SMEM)
    operands = (
        relax,
        time_index,
        stress,
        velocity,
        buoyancy,
        owner,
        cell,
        residual,
        lame,
        qinv,
        memory,
        fwd_strain,
    )
    dma = pltpu.SemaphoreType.DMA
    return pl.pallas_call(
        functools.partial(steps_kernel, n_tile, n_depth),
        out_shape=[
            jax.ShapeDtypeStruct(velocity.shape, f32),
            jax.ShapeDtypeStruct(stress.shape, f32),
            jax.ShapeDtypeStruct(memory.shape, f32),
            jax.ShapeDtypeStruct(buoyancy.shape, f32),
        ],
        in_specs=[smem_spec] * 2 + [any_spec] * 10,
        out_specs=[any_spec] * 4,
        scratch_shapes=[pltpu.VMEM(array.shape, array.dtype) for array in operands[2:]]
        + [
            pltpu.VMEM((2, cx, cz, ny), f32),
            pltpu.VMEM((6, cx, cz, ny), f32),
            pltpu.VMEM((cx, cz, ny), f32),
            pltpu.VMEM((cx + 2, 16, ny), f32),
            pltpu.VMEM((n_tile, 16, listed), f32),
            pltpu.VMEM((steps, 2, 7, cz, ny), f32),
            pltpu.VMEM((steps, 2, 7, cx, 1, ny), f32),
            pltpu.VMEM((steps, 2, 2, 5, 1, ny), f32),
            pltpu.VMEM((steps, 2, 7, cz, ny), f32),
            pltpu.VMEM((steps, 2, 7, cx, 1, ny), f32),
            pltpu.VMEM((steps, 2, 2, 5, 1, ny), f32),
            dma((10,)),
            dma((3 + mechs,)),
            dma((n_tile,)),
            dma((n_tile,)),
            dma((steps, 2)),
            dma((steps, 2)),
            dma((steps, 2)),
            dma((steps, 2)),
            dma((steps, 2, 2)),
            dma((steps, 2, 2)),
        ],
        compiler_params=pltpu.CompilerParams(
            collective_id=0, has_side_effects=True, vmem_limit_bytes=32 * 1024 * 1024
        ),
        cost_estimate=pl.CostEstimate(
            flops=800 * cx * cz * ny * steps, bytes_accessed=2600000, transcendentals=0
        ),
    )(*operands)


def solution(mesh):
    in_specs = (
        P(None, "tile", "depth", None),
        P(None, "tile", "depth", None),
        P(None, "tile", "depth", None),
        P("tile", "depth", None),
        P(None, "tile", "depth", None),
        P(None, "tile", "depth", None),
        P(),
        P(None, None, "tile", "depth", None),
        P(None, None, "tile"),
        P("tile", None),
        P("tile"),
        P(),
    )
    out_specs = (
        P(None, "tile", "depth", None),
        P(None, "tile", "depth", None),
        P(None, "tile", "depth", None),
        P("tile", "depth", None),
    )
    return jax.shard_map(
        functools.partial(per_device, mesh.shape["tile"], mesh.shape["depth"]),
        mesh=mesh,
        in_specs=in_specs,
        out_specs=out_specs,
        check_vma=False,
    )
```

```python
import functools

import jax
import jax.numpy as jnp
from jax import lax
from jax.experimental import pallas as pl
from jax.experimental.pallas import tpu as pltpu
from jax.sharding import PartitionSpec as P

courant = 0.2
mech_weights = (2.0, 3.0, 4.0)
MESH = pl.DeviceIdType.MESH

x_comps = (0, 3, 4)
z_comps = (4, 5, 2)
y_comps = (3, 1, 5)
corner_comps = (0, 3, 4, 5, 2)
step_of = (-1, 1)


def steps_kernel(
    n_tile,
    n_depth,
    relax_in,
    time_index_in,
    stress_in,
    velocity_in,
    buoyancy_in,
    owner_in,
    cell_in,
    residual_in,
    lame_in,
    qinv_in,
    memory_in,
    fwd_in,
    velocity,
    stress,
    memory,
    kern,
    buoyancy,
    owner,
    cell,
    residual,
    lame,
    qinv,
    fwd,
    relax,
    time_index,
    coef,
    force,
    sums,
    inject,
    gathered,
    xs,
    zs,
    cs,
    xr,
    zr,
    cr,
    in_sem,
    gs_sem,
    gr_sem,
    xs_sem,
    xr_sem,
    zs_sem,
    zr_sem,
    cs_sem,
    cr_sem,
):
    steps = fwd.shape[0]
    mechs = memory.shape[0] // 6
    cx, cz, ny = velocity.shape[1:]
    listed = owner.shape[1]
    blocks = gathered.shape[0]
    my_t = lax.axis_index("tile")
    my_d = lax.axis_index("depth")

    has_t = (my_t > 0, my_t < n_tile - 1)
    has_d = (my_d > 0, my_d < n_depth - 1)
    top = my_d == 0

    barrier = pltpu.get_barrier_semaphore()

    def greet(device, amount=1):
        pl.semaphore_signal(barrier, inc=amount, device_id=device, device_id_type=MESH)

    meets = []
    for other in range(2):
        meets.append((has_d[other], my_t, my_d + step_of[other]))
        for side in range(2):
            meets.append(
                (
                    jnp.logical_and(has_t[side], has_d[other]),
                    my_t + step_of[side],
                    my_d + step_of[other],
                )
            )
    for side in range(2):
        meets.append(
            (jnp.logical_and(has_t[side], jnp.logical_not(top)), my_t + step_of[side], my_d)
        )
    for here, to_t, to_d in meets:
        pl.when(here)(lambda: greet((to_t, to_d)))

    @pl.when(top)
    def _():
        for hop in range(1, n_tile):
            greet((lax.rem(my_t + hop, n_tile), my_d))

    loads = []
    for number, (src, dst) in enumerate(
        (
            (stress_in, stress),
            (velocity_in, velocity),
            (buoyancy_in, buoyancy),
            (owner_in, owner),
            (cell_in, cell),
            (residual_in, residual),
            (lame_in, lame),
            (qinv_in, qinv),
            (memory_in, memory),
            (fwd_in, fwd),
            (time_index_in, time_index),
            (relax_in, relax),
        )
    ):
        copy = pltpu.make_async_copy(src, dst, in_sem.at[number])
        copy.start()
        loads.append(copy)

    for side in range(2):

        @pl.when(jnp.logical_not(has_t[side]))
        def _():
            xr[:, side] = jnp.zeros((steps, 7, cz, ny), jnp.float32)

        @pl.when(jnp.logical_not(has_d[side]))
        def _():
            zr[:, side] = jnp.zeros((steps, 7, cx, 1, ny), jnp.float32)

        for other in range(2):

            @pl.when(jnp.logical_not(jnp.logical_and(has_t[side], has_d[other])))
            def _():
                cr[:, side, other] = jnp.zeros((steps, 5, 1, ny), jnp.float32)

    def gather_copy(block, hop):
        return pltpu.make_async_remote_copy(
            src_ref=gathered.at[block, 0],
            dst_ref=gathered.at[block, hop],
            send_sem=gs_sem.at[block, hop],
            recv_sem=gr_sem.at[block, hop],
            device_id=(lax.rem(my_t + hop, n_tile), my_d),
            device_id_type=MESH,
        )

    def x_copy(step, side, early):
        first, comps = (0, 3) if early else (3, 4 if step == 0 else 3)
        return pltpu.make_async_remote_copy(
            src_ref=xs.at[step, side, pl.ds(first, comps)],
            dst_ref=xr.at[step, 1 - side, pl.ds(first, comps)],
            send_sem=xs_sem.at[step, side, int(early)],
            recv_sem=xr_sem.at[step, 1 - side, int(early)],
            device_id=(my_t + step_of[side], my_d),
            device_id_type=MESH,
        )

    def z_copy(step, side):
        comps = 7 if step == 0 else 6
        return pltpu.make_async_remote_copy(
            src_ref=zs.at[step, side, pl.ds(0, comps)],
            dst_ref=zr.at[step, 1 - side, pl.ds(0, comps)],
            send_sem=zs_sem.at[step, side],
            recv_sem=zr_sem.at[step, 1 - side],
            device_id=(my_t, my_d + step_of[side]),
            device_id_type=MESH,
        )

    def corner_copy(step, side, other):
        return pltpu.make_async_remote_copy(
            src_ref=cs.at[step, side, other],
            dst_ref=cr.at[step, 1 - side, 1 - other],
            send_sem=cs_sem.at[step, side, other],
            recv_sem=cr_sem.at[step, 1 - side, 1 - other],
            device_id=(my_t + step_of[side], my_d + step_of[other]),
            device_id_type=MESH,
        )

    shape = (cx, cz, ny)
    at_z = lax.broadcasted_iota(jnp.int32, shape, 1)
    at_y = lax.broadcasted_iota(jnp.int32, shape, 2)
    z_first, z_last = at_z == 0, at_z == cz - 1
    y_first, y_last = at_y == 0, at_y == ny - 1
    ends_x = (0, cx - 1)
    ends_z = (0, cz - 1)

    def diff_y(field):
        after = jnp.where(y_last, 0.0, pltpu.roll(field, ny - 1, 2))
        before = jnp.where(y_first, 0.0, pltpu.roll(field, 1, 2))
        return after - before

    def diff_z(field, low, high):
        after = jnp.where(z_last, high, pltpu.roll(field, cz - 1, 1))
        before = jnp.where(z_first, low, pltpu.roll(field, 1, 1))
        return after - before

    def diff_x(field, low, high):
        return jnp.concatenate([field[1:], high], axis=0) - jnp.concatenate(
            [low, field[:-1]], axis=0
        )

    def send_corners(step):
        for side in range(2):
            for other in range(2):

                @pl.when(jnp.logical_and(has_t[side], has_d[other]))
                def _():
                    for slot, comp in enumerate(corner_comps):
                        cs[step, side, other, slot] = stress[
                            comp, ends_x[side], pl.ds(ends_z[other], 1), :
                        ]
                    corner_copy(step, side, other).start()

        for side in range(2):

            @pl.when(has_t[side])
            def _():
                for slot, comp in enumerate(x_comps):
                    xs[step, side, slot] = stress[comp, ends_x[side]]
                x_copy(step, side, True).start()

    def send_sides(step):
        scale = (0.5 * courant) * buoyancy[...]
        none_x = jnp.zeros((1, cz, ny), jnp.float32)
        for comp in range(3):
            sx = stress[x_comps[comp]]
            sz = stress[z_comps[comp]]
            change = (
                diff_x(sx, none_x, none_x)
                + diff_y(stress[y_comps[comp]])
                + diff_z(sz, 0.0, 0.0)
            )
            part = velocity[comp] + scale * change
            velocity[comp] = part
            for side in range(2):
                xs[step, side, 3 + comp] = part[ends_x[side]]
                end = ends_z[side]
                zs[step, side, comp] = part[:, end : end + 1, :]
                zs[step, side, 3 + comp] = sz[:, end : end + 1, :]
        if step == 0:
            for side in range(2):
                xs[step, side, 6] = scale[ends_x[side]]
                end = ends_z[side]
                zs[step, side, 6] = scale[:, end : end + 1, :]
        for side in range(2):
            pl.when(has_d[side])(lambda: z_copy(step, side).start())
            pl.when(has_t[side])(lambda: x_copy(step, side, False).start())

    def wait_halo(step):
        for side in range(2):
            pl.when(has_d[side])(lambda: z_copy(step, 1 - side).wait_recv())
            pl.when(has_t[side])(
                lambda: [x_copy(step, 1 - side, early).wait_recv() for early in (True, False)] and None
            )
            for other in range(2):
                pl.when(jnp.logical_and(has_t[side], has_d[other]))(
                    lambda: corner_copy(step, 1 - side, 1 - other).wait_recv()
                )

    def wait_sent(step):
        for side in range(2):
            pl.when(has_d[side])(lambda: z_copy(step, side).wait_send())
            pl.when(has_t[side])(
                lambda: [x_copy(step, side, early).wait_send() for early in (True, False)] and None
            )
            for other in range(2):
                pl.when(jnp.logical_and(has_t[side], has_d[other]))(
                    lambda: corner_copy(step, side, other).wait_send()
                )

    peers = jnp.where(top, n_tile - 1, 0)
    for here, _, _ in meets:
        peers = peers + jnp.where(here, 1, 0)
    pl.semaphore_wait(barrier, peers)

    for number in (3, 4, 5, 10):
        loads[number].wait()

    def send_stations(block):
        for hop in range(1, n_tile):
            gather_copy(block, hop).start()

    @pl.when(top)
    def _():
        gathered[:, 0] = jnp.zeros((blocks, 8, listed), jnp.float32)
        for step in range(steps):
            for comp in range(3):
                row = 3 * (step % 2) + comp
                gathered[step // 2, 0, row : row + 1] = residual[
                    comp, pl.ds(time_index[step], 1), :
                ]
        gathered[0, 0, 6:7] = (owner[...] * (cx * ny) + cell[...]).astype(jnp.float32)
        send_stations(0)

    loads[0].wait()
    send_corners(0)
    loads[1].wait()
    loads[2].wait()
    send_sides(0)

    @pl.when(top)
    def _():
        for block in range(1, blocks):
            send_stations(block)

    loads[6].wait()
    loads[7].wait()
    lam, shear = lame[0], lame[1]
    twist = 2.0 * shear
    shape_part = twist * qinv[0]
    bulk_part = (lam + (2.0 / 3.0) * shear) * qinv[1] - shape_part * (1.0 / 3.0)
    coef[0] = shape_part
    coef[1] = bulk_part
    kern[...] = jnp.zeros(shape, jnp.float32)

    def place_stations(block):
        for hop in range(1, n_tile):
            gather_copy(block, hop).wait_recv()
        rows = jnp.concatenate([gathered[block, hop] for hop in range(n_tile)], axis=1)
        target = jnp.concatenate([gathered[0, hop, 6:7] for hop in range(n_tile)], axis=1)
        target = target.astype(jnp.int32)
        total = n_tile * listed
        at_cell = lax.broadcasted_iota(jnp.int32, (ny, total), 0)
        hot = jnp.where(at_cell == lax.rem(target, ny), 1.0, 0.0).astype(jnp.bfloat16)
        local = target - (my_t * cx - 1) * ny
        high = rows.astype(jnp.bfloat16).astype(jnp.float32)
        rest = rows - high
        middle = rest.astype(jnp.bfloat16).astype(jnp.float32)
        low = rest - middle
        sides = []
        for part in (high, middle, low):
            for layer in range(cx + 2):
                inside = jnp.logical_and(local >= layer * ny, local < (layer + 1) * ny)
                sides.append(jnp.where(inside, part, 0.0))
        found = lax.dot_general(
            jnp.concatenate(sides, axis=0).astype(jnp.bfloat16),
            hot,
            (((1,), (1,)), ((), ())),
            preferred_element_type=jnp.float32,
        )
        third = (cx + 2) * 8
        found = found[:third] + found[third : 2 * third] + found[2 * third :]
        for layer in range(cx + 2):
            inject[layer, 8 * block : 8 * block + 8] = found[8 * layer : 8 * layer + 8]

    @pl.when(jnp.logical_not(top))
    def _():
        inject[...] = jnp.zeros((cx + 2, 8 * blocks, ny), jnp.float32)

    loads[8].wait()
    loads[9].wait()
    loads[11].wait()
    keeps = [1.0 - relax[mech] for mech in range(mechs)]
    pushes = [relax[mech] * mech_weights[mech] for mech in range(mechs)]
    push_all = pushes[0]
    for push in pushes[1:]:
        push_all = push_all + push


    for comp in range(6):
        total = keeps[0] * memory[comp]
        for mech in range(1, mechs):
            total = total + keeps[mech] * memory[6 * mech + comp]
        sums[comp] = total

    edge = lax.broadcasted_iota(jnp.int32, (1, cz, ny), 1)
    edge_ends = (edge == 0, edge == cz - 1)
    for step in range(steps):
        last = step == steps - 1
        for block in range(blocks):
            if step == max(0, 2 * block - 1):
                pl.when(top)(lambda: place_stations(block))
        wait_halo(step)

        scale = (0.5 * courant) * buoyancy[...]
        x_scale = [xr[0, side, 6] for side in range(2)]
        z_scale = [zr[0, side, 6] for side in range(2)]
        grads_x, grads_y, grads_z = [], [], []
        for comp in range(3):
            own = velocity[comp]
            row = 8 * (step // 2) + 3 * (step % 2) + comp
            signs = (-1.0, 1.0)
            around_x, around_z = [], []
            extra = []
            for side in range(2):
                sx_end = stress[x_comps[comp], ends_x[side]]
                halo = xr[step, side, 3 + comp] - signs[side] * x_scale[side] * sx_end
                fix = jnp.zeros((cz, ny), jnp.float32)
                for other in range(2):
                    at_corner = cr[step, side, other, corner_comps.index(z_comps[comp])]
                    fix = fix + jnp.where(edge_ends[other][0], signs[other] * at_corner, 0.0)
                push_in = inject[(0, cx + 1)[side], row : row + 1, :] * (2.0 / courant)
                fix = fix + jnp.where(edge_ends[0][0], push_in, 0.0)
                around_x.append((halo + x_scale[side] * fix)[None])
                extra.append((signs[side] * xr[step, side, comp])[None])

                sz_end = stress[z_comps[comp], :, pl.ds(ends_z[side], 1), :]
                corner_row = corner_comps.index(x_comps[comp])
                at_low = cr[step, 0, side, corner_row][None]
                at_high = cr[step, 1, side, corner_row][None]
                middle = jnp.zeros((cx - 2, 1, ny), jnp.float32)
                if cx > 1:
                    fix = jnp.concatenate([-at_low, middle, at_high], axis=0)
                else:
                    fix = at_high - at_low
                around_z.append(
                    zr[step, side, comp] + z_scale[side] * (fix - signs[side] * sz_end)
                )
            if cx > 1:
                change = jnp.concatenate(
                    [extra[0], jnp.zeros((cx - 2, cz, ny), jnp.float32), extra[1]], axis=0
                )
            else:
                change = extra[0] + extra[1]
            push_in = inject[1 : cx + 1, row : row + 1, :] * (2.0 / courant)
            change = change + jnp.where(z_first, push_in - zr[step, 0, 3 + comp], 0.0)
            change = change + jnp.where(z_last, zr[step, 1, 3 + comp], 0.0)
            own = own + scale * change
            velocity[comp] = own
            grads_x.append(diff_x(own, around_x[0], around_x[1]))
            grads_y.append(diff_y(own))
            grads_z.append(diff_z(own, around_z[0], around_z[1]))
        strain = [
            0.5 * grads_x[0],
            0.5 * grads_y[1],
            0.5 * grads_z[2],
            0.25 * (grads_y[0] + grads_x[1]),
            0.25 * (grads_z[0] + grads_x[2]),
            0.25 * (grads_z[1] + grads_y[2]),
        ]
        theta = strain[0] + strain[1] + strain[2]
        bulk = coef[1] * theta
        pressure = lame[0] * theta
        for comp in range(6):
            push = coef[0] * strain[comp]
            grow = 2.0 * lame[1] * strain[comp]
            if comp < 3:
                push = push + bulk
                grow = grow + pressure
            total = sums[comp] - push_all * push
            sums[comp] = total
            force[comp] = push
            stress[comp] = stress[comp] + courant * (grow + total)
        if not last:
            send_corners(step + 1)
            send_sides(step + 1)
        weighted = kern[...]
        for comp in range(6):
            weighted = weighted + sums[comp] * fwd[step, comp].astype(jnp.float32)
        kern[...] = courant * weighted if last else weighted
        for comp in range(6):
            push = force[comp]
            total = None
            for mech in range(mechs):
                index = 6 * mech + comp
                new = keeps[mech] * memory[index] - pushes[mech] * push
                memory[index] = new
                if not last:
                    ahead = keeps[mech] * new
                    total = ahead if total is None else total + ahead
            if not last:
                sums[comp] = total

    for step in range(steps):
        wait_sent(step)

    @pl.when(top)
    def _():
        for block in range(blocks):
            for hop in range(1, n_tile):
                gather_copy(block, hop).wait_send()


def hand_out(velocity, stress, memory, kern, velocity_to, stress_to, memory_to, kern_to, sem):
    copies = [
        pltpu.make_async_copy(src, dst, sem.at[number])
        for number, (src, dst) in enumerate(
            (
                (memory, memory_to),
                (stress, stress_to),
                (velocity, velocity_to),
                (kern, kern_to),
            )
        )
    ]
    for copy in copies:
        copy.start()
    for copy in copies:
        copy.wait()


def per_device(
    n_tile,
    n_depth,
    velocity,
    stress,
    memory,
    buoyancy,
    lame,
    qinv,
    relax,
    fwd_strain,
    residual,
    station_owner,
    station_cell,
    time_index,
):
    steps = fwd_strain.shape[0]
    mechs = relax.shape[0]
    cx, cz, ny = buoyancy.shape
    listed = station_cell.shape[0]
    f32 = jnp.float32
    blocks = -(-steps // 2)
    owner = station_owner.reshape(1, listed)
    cell = station_cell.reshape(1, listed)
    any_spec = pl.BlockSpec(memory_space=pl.ANY)
    arrays = (
        relax,
        time_index,
        stress,
        velocity,
        buoyancy,
        owner,
        cell,
        jnp.transpose(residual, (1, 0, 2)),
        lame,
        qinv,
        memory,
        fwd_strain,
    )
    arrays = [pltpu.with_memory_space_constraint(array, pltpu.HBM) for array in arrays]
    held = arrays[4:10] + arrays[11:]
    dma = pltpu.SemaphoreType.DMA
    results = (velocity, stress, memory, buoyancy)
    state = pl.pallas_call(
        functools.partial(steps_kernel, n_tile, n_depth),
        out_shape=[pltpu.VMEM(array.shape, f32) for array in results],
        in_specs=[any_spec] * 12,
        out_specs=[pl.BlockSpec(memory_space=pltpu.VMEM)] * 4,
        scratch_shapes=[pltpu.VMEM(array.shape, array.dtype) for array in held]
        + [
            pltpu.SMEM(relax.shape, f32),
            pltpu.SMEM(time_index.shape, jnp.int32),
            pltpu.VMEM((2, cx, cz, ny), f32),
            pltpu.VMEM((6, cx, cz, ny), f32),
            pltpu.VMEM((6, cx, cz, ny), f32),
            pltpu.VMEM((cx + 2, 8 * blocks, ny), f32),
            pltpu.VMEM((blocks, n_tile, 8, listed), f32),
            pltpu.VMEM((steps, 2, 7, cz, ny), f32),
            pltpu.VMEM((steps, 2, 7, cx, 1, ny), f32),
            pltpu.VMEM((steps, 2, 2, 5, 1, ny), f32),
            pltpu.VMEM((steps, 2, 7, cz, ny), f32),
            pltpu.VMEM((steps, 2, 7, cx, 1, ny), f32),
            pltpu.VMEM((steps, 2, 2, 5, 1, ny), f32),
            dma((12,)),
            dma((blocks, n_tile)),
            dma((blocks, n_tile)),
            dma((steps, 2, 2)),
            dma((steps, 2, 2)),
            dma((steps, 2)),
            dma((steps, 2)),
            dma((steps, 2, 2)),
            dma((steps, 2, 2)),
        ],
        compiler_params=pltpu.CompilerParams(
            collective_id=0, has_side_effects=True, vmem_limit_bytes=32 * 1024 * 1024
        ),
        cost_estimate=pl.CostEstimate(
            flops=800 * cx * cz * ny * steps, bytes_accessed=2600000, transcendentals=0
        ),
    )(*arrays)
    return pl.pallas_call(
        hand_out,
        out_shape=[pltpu.HBM(array.shape, f32) for array in results],
        in_specs=[pl.BlockSpec(memory_space=pltpu.VMEM)] * 4,
        out_specs=[any_spec] * 4,
        scratch_shapes=[dma((4,))],
    )(*[pltpu.with_memory_space_constraint(array, pltpu.VMEM) for array in state])


def solution(mesh):
    in_specs = (
        P(None, "tile", "depth", None),
        P(None, "tile", "depth", None),
        P(None, "tile", "depth", None),
        P("tile", "depth", None),
        P(None, "tile", "depth", None),
        P(None, "tile", "depth", None),
        P(),
        P(None, None, "tile", "depth", None),
        P(None, None, "tile"),
        P("tile", None),
        P("tile"),
        P(),
    )
    out_specs = (
        P(None, "tile", "depth", None),
        P(None, "tile", "depth", None),
        P(None, "tile", "depth", None),
        P("tile", "depth", None),
    )
    return jax.shard_map(
        functools.partial(per_device, mesh.shape["tile"], mesh.shape["depth"]),
        mesh=mesh,
        in_specs=in_specs,
        out_specs=out_specs,
        check_vma=False,
    )
```

```python
import functools

import jax
import jax.numpy as jnp
from jax import lax
from jax.experimental import pallas as pl
from jax.experimental.pallas import tpu as pltpu
from jax.sharding import PartitionSpec as P

courant = 0.2
mech_weights = (2.0, 3.0, 4.0)
MESH = pl.DeviceIdType.MESH

x_comps = (0, 3, 4)
z_comps = (4, 5, 2)
y_comps = (3, 1, 5)
corner_comps = (0, 3, 4, 5, 2)
step_of = (-1, 1)


def steps_kernel(
    n_tile,
    n_depth,
    relax_in,
    time_index_in,
    stress_in,
    velocity_in,
    buoyancy_in,
    owner_in,
    cell_in,
    residual_in,
    lame_in,
    qinv_in,
    memory_in,
    fwd_in,
    velocity,
    stress,
    memory,
    kern,
    buoyancy,
    owner,
    cell,
    residual,
    lame,
    qinv,
    fwd,
    relax,
    time_index,
    coef,
    force,
    sums,
    inject,
    gathered,
    xs,
    zs,
    cs,
    xr,
    zr,
    cr,
    in_sem,
    gs_sem,
    gr_sem,
    xs_sem,
    xr_sem,
    zs_sem,
    zr_sem,
    cs_sem,
    cr_sem,
):
    steps = fwd.shape[0]
    mechs = memory.shape[0] // 6
    cx, cz, ny = velocity.shape[1:]
    listed = owner.shape[1]
    blocks = gathered.shape[0]
    my_t = lax.axis_index("tile")
    my_d = lax.axis_index("depth")

    loads = []
    for number, (src, dst) in enumerate(
        (
            (stress_in, stress),
            (velocity_in, velocity),
            (buoyancy_in, buoyancy),
            (owner_in, owner),
            (cell_in, cell),
            (residual_in, residual),
            (lame_in, lame),
            (qinv_in, qinv),
            (memory_in, memory),
            (fwd_in, fwd),
            (time_index_in, time_index),
            (relax_in, relax),
        )
    ):
        copy = pltpu.make_async_copy(src, dst, in_sem.at[number])
        if number < 3:
            copy.start()
        loads.append(copy)

    has_t = (my_t > 0, my_t < n_tile - 1)
    has_d = (my_d > 0, my_d < n_depth - 1)
    top = my_d == 0

    barrier = pltpu.get_barrier_semaphore()

    def greet(device, amount=1):
        pl.semaphore_signal(barrier, inc=amount, device_id=device, device_id_type=MESH)

    meets = []
    for other in range(2):
        meets.append((has_d[other], my_t, my_d + step_of[other]))
        for side in range(2):
            meets.append(
                (
                    jnp.logical_and(has_t[side], has_d[other]),
                    my_t + step_of[side],
                    my_d + step_of[other],
                )
            )
    for side in range(2):
        meets.append(
            (jnp.logical_and(has_t[side], jnp.logical_not(top)), my_t + step_of[side], my_d)
        )
    for here, to_t, to_d in meets:
        pl.when(here)(lambda: greet((to_t, to_d)))

    @pl.when(top)
    def _():
        for hop in range(1, n_tile):
            greet((lax.rem(my_t + hop, n_tile), my_d))

    for number in (3, 4, 5, 10, 11, 6, 7, 8, 9):
        loads[number].start()

    for side in range(2):

        @pl.when(jnp.logical_not(has_t[side]))
        def _():
            xr[:, side] = jnp.zeros((steps, 7, cz, ny), jnp.float32)

        @pl.when(jnp.logical_not(has_d[side]))
        def _():
            zr[:, side] = jnp.zeros((steps, 7, cx, 1, ny), jnp.float32)

        for other in range(2):

            @pl.when(jnp.logical_not(jnp.logical_and(has_t[side], has_d[other])))
            def _():
                cr[:, side, other] = jnp.zeros((steps, 5, 1, ny), jnp.float32)

    def gather_copy(block, hop):
        return pltpu.make_async_remote_copy(
            src_ref=gathered.at[block, 0],
            dst_ref=gathered.at[block, hop],
            send_sem=gs_sem.at[block, hop],
            recv_sem=gr_sem.at[block, hop],
            device_id=(lax.rem(my_t + hop, n_tile), my_d),
            device_id_type=MESH,
        )

    def x_copy(step, side, early):
        first, comps = (0, 3) if early else (3, 4 if step == 0 else 3)
        return pltpu.make_async_remote_copy(
            src_ref=xs.at[step, side, pl.ds(first, comps)],
            dst_ref=xr.at[step, 1 - side, pl.ds(first, comps)],
            send_sem=xs_sem.at[step, side, int(early)],
            recv_sem=xr_sem.at[step, 1 - side, int(early)],
            device_id=(my_t + step_of[side], my_d),
            device_id_type=MESH,
        )

    def z_copy(step, side):
        comps = 7 if step == 0 else 6
        return pltpu.make_async_remote_copy(
            src_ref=zs.at[step, side, pl.ds(0, comps)],
            dst_ref=zr.at[step, 1 - side, pl.ds(0, comps)],
            send_sem=zs_sem.at[step, side],
            recv_sem=zr_sem.at[step, 1 - side],
            device_id=(my_t, my_d + step_of[side]),
            device_id_type=MESH,
        )

    def corner_copy(step, side, other):
        return pltpu.make_async_remote_copy(
            src_ref=cs.at[step, side, other],
            dst_ref=cr.at[step, 1 - side, 1 - other],
            send_sem=cs_sem.at[step, side, other],
            recv_sem=cr_sem.at[step, 1 - side, 1 - other],
            device_id=(my_t + step_of[side], my_d + step_of[other]),
            device_id_type=MESH,
        )

    shape = (cx, cz, ny)
    at_z = lax.broadcasted_iota(jnp.int32, shape, 1)
    at_y = lax.broadcasted_iota(jnp.int32, shape, 2)
    z_first, z_last = at_z == 0, at_z == cz - 1
    y_first, y_last = at_y == 0, at_y == ny - 1
    ends_x = (0, cx - 1)
    ends_z = (0, cz - 1)

    def diff_y(field):
        after = jnp.where(y_last, 0.0, pltpu.roll(field, ny - 1, 2))
        before = jnp.where(y_first, 0.0, pltpu.roll(field, 1, 2))
        return after - before

    def diff_z(field, low, high):
        after = jnp.where(z_last, high, pltpu.roll(field, cz - 1, 1))
        before = jnp.where(z_first, low, pltpu.roll(field, 1, 1))
        return after - before

    def diff_x(field, low, high):
        return jnp.concatenate([field[1:], high], axis=0) - jnp.concatenate(
            [low, field[:-1]], axis=0
        )

    def send_corners(step):
        for side in range(2):
            for other in range(2):

                @pl.when(jnp.logical_and(has_t[side], has_d[other]))
                def _():
                    for slot, comp in enumerate(corner_comps):
                        cs[step, side, other, slot] = stress[
                            comp, ends_x[side], pl.ds(ends_z[other], 1), :
                        ]
                    corner_copy(step, side, other).start()

        for side in range(2):

            @pl.when(has_t[side])
            def _():
                for slot, comp in enumerate(x_comps):
                    xs[step, side, slot] = stress[comp, ends_x[side]]
                x_copy(step, side, True).start()

    def send_sides(step):
        scale = (0.5 * courant) * buoyancy[...]
        none_x = jnp.zeros((1, cz, ny), jnp.float32)
        for comp in range(3):
            sx = stress[x_comps[comp]]
            sz = stress[z_comps[comp]]
            change = (
                diff_x(sx, none_x, none_x)
                + diff_y(stress[y_comps[comp]])
                + diff_z(sz, 0.0, 0.0)
            )
            part = velocity[comp] + scale * change
            velocity[comp] = part
            for side in range(2):
                xs[step, side, 3 + comp] = part[ends_x[side]]
                end = ends_z[side]
                zs[step, side, comp] = part[:, end : end + 1, :]
                zs[step, side, 3 + comp] = sz[:, end : end + 1, :]
        if step == 0:
            for side in range(2):
                xs[step, side, 6] = scale[ends_x[side]]
                end = ends_z[side]
                zs[step, side, 6] = scale[:, end : end + 1, :]
        for side in range(2):
            pl.when(has_d[side])(lambda: z_copy(step, side).start())
            pl.when(has_t[side])(lambda: x_copy(step, side, False).start())

    def wait_halo(step):
        for side in range(2):
            pl.when(has_d[side])(lambda: z_copy(step, 1 - side).wait_recv())
            pl.when(has_t[side])(
                lambda: [x_copy(step, 1 - side, early).wait_recv() for early in (True, False)] and None
            )
            for other in range(2):
                pl.when(jnp.logical_and(has_t[side], has_d[other]))(
                    lambda: corner_copy(step, 1 - side, 1 - other).wait_recv()
                )

    def wait_sent(step):
        for side in range(2):
            pl.when(has_d[side])(lambda: z_copy(step, side).wait_send())
            pl.when(has_t[side])(
                lambda: [x_copy(step, side, early).wait_send() for early in (True, False)] and None
            )
            for other in range(2):
                pl.when(jnp.logical_and(has_t[side], has_d[other]))(
                    lambda: corner_copy(step, side, other).wait_send()
                )

    peers = jnp.where(top, n_tile - 1, 0)
    for here, _, _ in meets:
        peers = peers + jnp.where(here, 1, 0)
    pl.semaphore_wait(barrier, peers)

    for number in (3, 4, 5, 10):
        loads[number].wait()

    def send_stations(block):
        for hop in range(1, n_tile):
            gather_copy(block, hop).start()

    @pl.when(top)
    def _():
        gathered[:, 0] = jnp.zeros((blocks, 8, listed), jnp.float32)
        for step in range(steps):
            for comp in range(3):
                row = 3 * (step % 2) + comp
                gathered[step // 2, 0, row : row + 1] = residual[
                    comp, pl.ds(time_index[step], 1), :
                ]
        gathered[0, 0, 6:7] = (owner[...] * (cx * ny) + cell[...]).astype(jnp.float32)
        send_stations(0)

    loads[0].wait()
    send_corners(0)
    loads[1].wait()
    loads[2].wait()
    send_sides(0)

    @pl.when(top)
    def _():
        for block in range(1, blocks):
            send_stations(block)

    loads[6].wait()
    loads[7].wait()
    lam, shear = lame[0], lame[1]
    twist = 2.0 * shear
    shape_part = twist * qinv[0]
    bulk_part = (lam + (2.0 / 3.0) * shear) * qinv[1] - shape_part * (1.0 / 3.0)
    coef[0] = shape_part
    coef[1] = bulk_part
    kern[...] = jnp.zeros(shape, jnp.float32)

    def place_stations(block):
        for hop in range(1, n_tile):
            gather_copy(block, hop).wait_recv()
        rows = jnp.concatenate([gathered[block, hop] for hop in range(n_tile)], axis=1)
        target = jnp.concatenate([gathered[0, hop, 6:7] for hop in range(n_tile)], axis=1)
        target = target.astype(jnp.int32)
        total = n_tile * listed
        at_cell = lax.broadcasted_iota(jnp.int32, (ny, total), 0)
        hot = jnp.where(at_cell == lax.rem(target, ny), 1.0, 0.0).astype(jnp.bfloat16)
        local = target - (my_t * cx - 1) * ny
        high = rows.astype(jnp.bfloat16).astype(jnp.float32)
        rest = rows - high
        middle = rest.astype(jnp.bfloat16).astype(jnp.float32)
        low = rest - middle
        sides = []
        for part in (high, middle, low):
            for layer in range(cx + 2):
                inside = jnp.logical_and(local >= layer * ny, local < (layer + 1) * ny)
                sides.append(jnp.where(inside, part, 0.0))
        found = lax.dot_general(
            jnp.concatenate(sides, axis=0).astype(jnp.bfloat16),
            hot,
            (((1,), (1,)), ((), ())),
            preferred_element_type=jnp.float32,
        )
        third = (cx + 2) * 8
        found = found[:third] + found[third : 2 * third] + found[2 * third :]
        for layer in range(cx + 2):
            inject[layer, 8 * block : 8 * block + 8] = found[8 * layer : 8 * layer + 8]

    @pl.when(jnp.logical_not(top))
    def _():
        inject[...] = jnp.zeros((cx + 2, 8 * blocks, ny), jnp.float32)

    loads[8].wait()
    loads[9].wait()
    loads[11].wait()
    keeps = [1.0 - relax[mech] for mech in range(mechs)]
    pushes = [relax[mech] * mech_weights[mech] for mech in range(mechs)]
    push_all = pushes[0]
    for push in pushes[1:]:
        push_all = push_all + push


    for comp in range(6):
        total = keeps[0] * memory[comp]
        for mech in range(1, mechs):
            total = total + keeps[mech] * memory[6 * mech + comp]
        sums[comp] = total

    edge = lax.broadcasted_iota(jnp.int32, (1, cz, ny), 1)
    edge_ends = (edge == 0, edge == cz - 1)
    for step in range(steps):
        last = step == steps - 1
        for block in range(blocks):
            if step == max(0, 2 * block - 1):
                pl.when(top)(lambda: place_stations(block))
        wait_halo(step)

        scale = (0.5 * courant) * buoyancy[...]
        x_scale = [xr[0, side, 6] for side in range(2)]
        z_scale = [zr[0, side, 6] for side in range(2)]
        grads_x, grads_y, grads_z = [], [], []
        for comp in range(3):
            own = velocity[comp]
            row = 8 * (step // 2) + 3 * (step % 2) + comp
            signs = (-1.0, 1.0)
            around_x, around_z = [], []
            extra = []
            for side in range(2):
                sx_end = stress[x_comps[comp], ends_x[side]]
                halo = xr[step, side, 3 + comp] - signs[side] * x_scale[side] * sx_end
                fix = jnp.zeros((cz, ny), jnp.float32)
                for other in range(2):
                    at_corner = cr[step, side, other, corner_comps.index(z_comps[comp])]
                    fix = fix + jnp.where(edge_ends[other][0], signs[other] * at_corner, 0.0)
                push_in = inject[(0, cx + 1)[side], row : row + 1, :] * (2.0 / courant)
                fix = fix + jnp.where(edge_ends[0][0], push_in, 0.0)
                around_x.append((halo + x_scale[side] * fix)[None])
                extra.append((signs[side] * xr[step, side, comp])[None])

                sz_end = stress[z_comps[comp], :, pl.ds(ends_z[side], 1), :]
                corner_row = corner_comps.index(x_comps[comp])
                at_low = cr[step, 0, side, corner_row][None]
                at_high = cr[step, 1, side, corner_row][None]
                middle = jnp.zeros((cx - 2, 1, ny), jnp.float32)
                if cx > 1:
                    fix = jnp.concatenate([-at_low, middle, at_high], axis=0)
                else:
                    fix = at_high - at_low
                around_z.append(
                    zr[step, side, comp] + z_scale[side] * (fix - signs[side] * sz_end)
                )
            if cx > 1:
                change = jnp.concatenate(
                    [extra[0], jnp.zeros((cx - 2, cz, ny), jnp.float32), extra[1]], axis=0
                )
            else:
                change = extra[0] + extra[1]
            push_in = inject[1 : cx + 1, row : row + 1, :] * (2.0 / courant)
            change = change + jnp.where(z_first, push_in - zr[step, 0, 3 + comp], 0.0)
            change = change + jnp.where(z_last, zr[step, 1, 3 + comp], 0.0)
            own = own + scale * change
            velocity[comp] = own
            grads_x.append(diff_x(own, around_x[0], around_x[1]))
            grads_y.append(diff_y(own))
            grads_z.append(diff_z(own, around_z[0], around_z[1]))
        strain = [
            0.5 * grads_x[0],
            0.5 * grads_y[1],
            0.5 * grads_z[2],
            0.25 * (grads_y[0] + grads_x[1]),
            0.25 * (grads_z[0] + grads_x[2]),
            0.25 * (grads_z[1] + grads_y[2]),
        ]
        theta = strain[0] + strain[1] + strain[2]
        bulk = coef[1] * theta
        pressure = lame[0] * theta
        for comp in range(6):
            push = coef[0] * strain[comp]
            grow = 2.0 * lame[1] * strain[comp]
            if comp < 3:
                push = push + bulk
                grow = grow + pressure
            total = sums[comp] - push_all * push
            sums[comp] = total
            force[comp] = push
            stress[comp] = stress[comp] + courant * (grow + total)
        if not last:
            send_corners(step + 1)
            send_sides(step + 1)
        weighted = kern[...]
        for comp in range(6):
            weighted = weighted + sums[comp] * fwd[step, comp].astype(jnp.float32)
        kern[...] = courant * weighted if last else weighted
        for comp in range(6):
            push = force[comp]
            total = None
            for mech in range(mechs):
                index = 6 * mech + comp
                new = keeps[mech] * memory[index] - pushes[mech] * push
                memory[index] = new
                if not last:
                    ahead = keeps[mech] * new
                    total = ahead if total is None else total + ahead
            if not last:
                sums[comp] = total

    for step in range(steps):
        wait_sent(step)

    @pl.when(top)
    def _():
        for block in range(blocks):
            for hop in range(1, n_tile):
                gather_copy(block, hop).wait_send()


def hand_out(velocity, stress, memory, kern, velocity_to, stress_to, memory_to, kern_to, sem):
    pairs = []
    for first in range(0, memory.shape[0], 3):
        rows = pl.ds(first, 3)
        pairs.append((memory.at[rows], memory_to.at[rows]))
    for first in (0, 3):
        rows = pl.ds(first, 3)
        pairs.append((stress.at[rows], stress_to.at[rows]))
    pairs.append((velocity, velocity_to))
    pairs.append((kern, kern_to))
    copies = [
        pltpu.make_async_copy(src, dst, sem.at[number])
        for number, (src, dst) in enumerate(pairs)
    ]
    for copy in copies:
        copy.start()
    for copy in copies:
        copy.wait()


def per_device(
    n_tile,
    n_depth,
    velocity,
    stress,
    memory,
    buoyancy,
    lame,
    qinv,
    relax,
    fwd_strain,
    residual,
    station_owner,
    station_cell,
    time_index,
):
    steps = fwd_strain.shape[0]
    mechs = relax.shape[0]
    cx, cz, ny = buoyancy.shape
    listed = station_cell.shape[0]
    f32 = jnp.float32
    blocks = -(-steps // 2)
    owner = station_owner.reshape(1, listed)
    cell = station_cell.reshape(1, listed)
    any_spec = pl.BlockSpec(memory_space=pl.ANY)
    arrays = (
        relax,
        time_index,
        stress,
        velocity,
        buoyancy,
        owner,
        cell,
        jnp.transpose(residual, (1, 0, 2)),
        lame,
        qinv,
        memory,
        fwd_strain,
    )
    arrays = [pltpu.with_memory_space_constraint(array, pltpu.HBM) for array in arrays]
    held = arrays[4:10] + arrays[11:]
    dma = pltpu.SemaphoreType.DMA
    results = (velocity, stress, memory, buoyancy)
    state = pl.pallas_call(
        functools.partial(steps_kernel, n_tile, n_depth),
        out_shape=[pltpu.VMEM(array.shape, f32) for array in results],
        in_specs=[any_spec] * 12,
        out_specs=[pl.BlockSpec(memory_space=pltpu.VMEM)] * 4,
        scratch_shapes=[pltpu.VMEM(array.shape, array.dtype) for array in held]
        + [
            pltpu.SMEM(relax.shape, f32),
            pltpu.SMEM(time_index.shape, jnp.int32),
            pltpu.VMEM((2, cx, cz, ny), f32),
            pltpu.VMEM((6, cx, cz, ny), f32),
            pltpu.VMEM((6, cx, cz, ny), f32),
            pltpu.VMEM((cx + 2, 8 * blocks, ny), f32),
            pltpu.VMEM((blocks, n_tile, 8, listed), f32),
            pltpu.VMEM((steps, 2, 7, cz, ny), f32),
            pltpu.VMEM((steps, 2, 7, cx, 1, ny), f32),
            pltpu.VMEM((steps, 2, 2, 5, 1, ny), f32),
            pltpu.VMEM((steps, 2, 7, cz, ny), f32),
            pltpu.VMEM((steps, 2, 7, cx, 1, ny), f32),
            pltpu.VMEM((steps, 2, 2, 5, 1, ny), f32),
            dma((12,)),
            dma((blocks, n_tile)),
            dma((blocks, n_tile)),
            dma((steps, 2, 2)),
            dma((steps, 2, 2)),
            dma((steps, 2)),
            dma((steps, 2)),
            dma((steps, 2, 2)),
            dma((steps, 2, 2)),
        ],
        compiler_params=pltpu.CompilerParams(
            collective_id=0, has_side_effects=True, vmem_limit_bytes=32 * 1024 * 1024
        ),
        cost_estimate=pl.CostEstimate(
            flops=800 * cx * cz * ny * steps, bytes_accessed=2600000, transcendentals=0
        ),
    )(*arrays)
    return pl.pallas_call(
        hand_out,
        out_shape=[pltpu.HBM(array.shape, f32) for array in results],
        in_specs=[pl.BlockSpec(memory_space=pltpu.VMEM)] * 4,
        out_specs=[any_spec] * 4,
        scratch_shapes=[dma((2 * mechs + 4,))],
    )(*[pltpu.with_memory_space_constraint(array, pltpu.VMEM) for array in state])


def solution(mesh):
    in_specs = (
        P(None, "tile", "depth", None),
        P(None, "tile", "depth", None),
        P(None, "tile", "depth", None),
        P("tile", "depth", None),
        P(None, "tile", "depth", None),
        P(None, "tile", "depth", None),
        P(),
        P(None, None, "tile", "depth", None),
        P(None, None, "tile"),
        P("tile", None),
        P("tile"),
        P(),
    )
    out_specs = (
        P(None, "tile", "depth", None),
        P(None, "tile", "depth", None),
        P(None, "tile", "depth", None),
        P("tile", "depth", None),
    )
    return jax.shard_map(
        functools.partial(per_device, mesh.shape["tile"], mesh.shape["depth"]),
        mesh=mesh,
        in_specs=in_specs,
        out_specs=out_specs,
        check_vma=False,
    )
```
